32 devices in a mesh: cell: 8 (over z, y), gene: 4 (over x, core).
Axes of the slice: x: 2, y: 2, z: 4, core: 2. Of those that a mesh axis runs over, the one named last changes fastest.
Arguments:
- expression: bfloat16 [65536, 512], P('cell', 'gene'), may hold values from 0 to 9, as said below
- affinity: bfloat16 [448, 256, 256], P('cell', 'gene'), may hold values from 0 to 1, as said below
- tile_rows: int32 [448], P('cell'), may hold values from 0 to 255, as said below
- tile_cols: int32 [448], P('cell'), may hold values from 0 to 255, as said below
- tile_count: int32 [8], P('cell'), may hold values from 35 to 53, as said below
Outputs:
- imputed: float32 [65536, 512], P('cell', 'gene')
The draws below stay inside these ranges and needn't reach their ends.
Inputs may be any that keep to these rules, and one draw needn't show every extreme that they name: `tile_rows`: the slots of index d of cell hold row blocks d * 32 to (d + 1) * 32 - 1. Among its first tile_count[d] slots each of those row blocks appears exactly once with itself as column block, and every other such slot names a column block of another index of cell. `tile_cols`: among the slots in use of one index of cell at most 3 name column blocks of any one other index, and on every index exactly 3 name those of some other index. A pair of blocks may repeat. `tile_count`: both ends are reached in every draw. `expression`: Positive. `affinity`: Positive.
All inputs are finite; a program needn't handle non-finite values.
Results may differ from the reference program's by a relative error of at most 0.0027.
Values may be sent and summed in bfloat16 or wider, within the bound.
A program may use at most 192 MiB of HBM per device.

```python
import math
import jax
import jax.numpy as jnp
from jax import lax

G = 512
BS = 256
BLK_DEV = 32
REQ_CAP = 3
STEPS = 3
TILE_DEV = 56
BLOCKS = 256
CELLS = 65536
TILES = 448
N_CELL = 8


def tile_plan(key):
    base = jax.random.fold_in(key, 101)
    keys = jax.random.split(base, 7)
    device = jnp.arange(N_CELL, dtype=jnp.int32)
    full_dev = jax.random.randint(keys[6], (), 0, N_CELL)
    lean_dev = (full_dev + 1) % N_CELL
    upper = jax.random.randint(keys[0], (N_CELL, 1), 2, REQ_CAP + 1)
    per_peer = jnp.minimum(jax.random.randint(keys[1], (N_CELL, N_CELL), 0, REQ_CAP + 1), upper)
    per_peer = jnp.where((device == full_dev)[:, None], REQ_CAP, per_peer)
    per_peer = jnp.where((device == lean_dev)[:, None], 0, per_peer)
    forced = (device + 1 + jax.random.randint(keys[2], (N_CELL,), 0, N_CELL - 1)) % N_CELL
    per_peer = jnp.where(device[None, :] == forced[:, None], REQ_CAP, per_peer)
    per_peer = jnp.where(device[None, :] == device[:, None], 0, per_peer)
    place = jnp.arange(REQ_CAP, dtype=jnp.int32)
    live = (place[None, None, :] < per_peer[:, :, None]).reshape(N_CELL, N_CELL * REQ_CAP)
    peer = jnp.broadcast_to(device[None, :, None], (N_CELL, N_CELL, REQ_CAP)).reshape(N_CELL, N_CELL * REQ_CAP)
    col_slot = jax.random.randint(keys[3], (N_CELL, N_CELL * REQ_CAP), 0, BLK_DEV)
    row_slot = jax.random.randint(keys[4], (N_CELL, N_CELL * REQ_CAP), 0, BLK_DEV)
    far_cols = peer * BLK_DEV + col_slot
    far_rows = device[:, None] * BLK_DEV + row_slot
    own = device[:, None] * BLK_DEV + jnp.arange(BLK_DEV, dtype=jnp.int32)[None, :]
    cols = jnp.concatenate([own, far_cols], axis=1)
    rows = jnp.concatenate([own, far_rows], axis=1)
    valid = jnp.concatenate([jnp.ones((N_CELL, BLK_DEV), dtype=bool), live], axis=1)
    width = BLK_DEV + N_CELL * REQ_CAP
    index = jnp.arange(width, dtype=jnp.int32)[None, :]
    score = jax.random.randint(keys[5], (N_CELL, width), 0, width) * width + index
    score = jnp.where(valid, score, width * width + index)
    order = jnp.argsort(score, axis=1, stable=True)
    rows = jnp.take_along_axis(rows, order, axis=1)
    cols = jnp.take_along_axis(cols, order, axis=1)
    count = jnp.sum(valid.astype(jnp.int32), axis=1)
    return (rows.reshape(-1).astype(jnp.int32), cols.reshape(-1).astype(jnp.int32), count.astype(jnp.int32))


def draw_tile_rows(key, part):
    return tile_plan(key)[0]


def draw_tile_cols(key, part):
    return tile_plan(key)[1]


def draw_tile_count(key, part):
    return tile_plan(key)[2]


def draw_affinity(key, part):
    uniform_part = jax.random.uniform(jax.random.fold_in(key, 13), (TILES, BS, BS), jnp.float32, 0.0, 1.0)
    values = 0.001 + 0.999 * uniform_part ** 200.0
    return values.astype(jnp.bfloat16)


def draw_expression(key, part):
    first, second = jax.random.split(jax.random.fold_in(key, 7))
    block_scale = jnp.exp(jax.random.uniform(first, (BLOCKS, 1, G), jnp.float32, math.log(0.3), math.log(3.0)))
    noise = jnp.exp(jax.random.uniform(second, (BLOCKS, BS, G), jnp.float32, math.log(0.01), 0.0))
    rise = 1.0 + 2.0 * jnp.arange(BLOCKS, dtype=jnp.float32) / BLOCKS
    values = block_scale * noise * rise[:, None, None]
    return values.reshape(BLOCKS * BS, G).astype(jnp.bfloat16)


def setup_inputs(seed: int = 0) -> dict:
    arg_keys = jax.random.split(jax.random.key(seed), 6)
    expression = draw_expression(jax.random.fold_in(arg_keys[5], 71), 0)
    affinity = draw_affinity(jax.random.fold_in(arg_keys[5], 71), 0)
    tile_rows = draw_tile_rows(jax.random.fold_in(arg_keys[5], 71), 0)
    tile_cols = draw_tile_cols(jax.random.fold_in(arg_keys[5], 71), 0)
    tile_count = draw_tile_count(jax.random.fold_in(arg_keys[5], 71), 0)
    return {"expression": expression, "affinity": affinity, "tile_rows": tile_rows, "tile_cols": tile_cols, "tile_count": tile_count}


def reference(expression, affinity, tile_rows, tile_cols, tile_count):
    tiles = affinity.reshape(N_CELL, TILE_DEV, BS, BS)
    rows = tile_rows.reshape(N_CELL, TILE_DEV)
    cols = tile_cols.reshape(N_CELL, TILE_DEV)
    owners = jnp.arange(N_CELL, dtype=jnp.int32)
    eye = jnp.eye(BS, dtype=bool)

    def prepare(device_tiles, device_rows, device_cols, count):
        valid = jnp.arange(TILE_DEV, dtype=jnp.int32) < count
        selfish = (device_rows == device_cols)[:, None, None] & eye[None]
        keep = valid[:, None, None] & jnp.logical_not(selfish)
        return jnp.where(keep, device_tiles, jnp.zeros_like(device_tiles))

    def one_step(current, final):
        def per_device(item):
            device_tiles, device_rows, device_cols, count, owner = item
            masked = prepare(device_tiles, device_rows, device_cols, count)
            local_row = (device_rows - owner * BLK_DEV).astype(jnp.int32)
            sums = jnp.sum(masked.astype(jnp.float32), axis=-1)
            degree = jax.ops.segment_sum(sums, local_row, BLK_DEV)
            operand = current[device_cols].astype(jnp.float32)
            product = jnp.einsum("tij,tjg->tig", masked.astype(jnp.float32), operand)
            total = jax.ops.segment_sum(product, local_row, BLK_DEV)
            return total / degree[:, :, None]

        out = lax.map(per_device, (tiles, rows, cols, tile_count, owners))
        out = out.reshape(BLOCKS, BS, G)
        if final:
            return out
        return out.astype(jnp.bfloat16)

    current = expression.reshape(BLOCKS, BS, G)
    for step in range(STEPS):
        current = one_step(current, step == STEPS - 1)
    last = current.reshape(CELLS, G)
    top_start = jnp.max(expression.astype(jnp.float32), axis=0)
    top_end = jnp.max(last, axis=0)
    return last * (top_start / top_end)[None, :]
```

```python
import functools
import jax
import jax.numpy as jnp
from jax import lax
from jax.experimental import pallas as pl
from jax.experimental.pallas import tpu as pltpu
from jax.sharding import PartitionSpec as P

BS = 256
BLK_DEV = 32
REQ_CAP = 3
STEPS = 3
MESH = pl.DeviceIdType.MESH


def spans(first, last, size):
    return [(at, min(size, last - at)) for at in range(first, last, size)]


def kernel(
    n, meta, wanted, x_ref, aff, last_hbm, ratio,
    a_full, cur, total, deg, chain, inc, out, asked_v, asked_s, tops, tops_in,
    req_send, req_recv, x_send, x_recv, a_send, a_recv, top_send, top_recv, local_sem, hbm_sem,
):
    far = n - 1
    links = far * REQ_CAP
    slots = BLK_DEV + links
    prev_at = slots
    last_at = slots + links
    chunks = spans(0, BLK_DEV, 8) + spans(BLK_DEV, slots, max(7, links // 4))
    me = lax.axis_index("cell")
    g = lax.axis_index("gene")
    across = lax.rem(g + 2, 4)
    sister = g + 1 - 2 * lax.rem(g, 2)
    rows = aff.shape[1]

    def after(d):
        return lax.rem(me + d, n)

    def before(d):
        return lax.rem(me + n - d, n)

    barrier = pltpu.get_barrier_semaphore()

    def greet(d, carry):
        pl.semaphore_signal(barrier, inc=1, device_id={"cell": after(d)}, device_id_type=MESH)
        return carry

    lax.fori_loop(1, n, greet, 0)
    for other in (across, sister):
        pl.semaphore_signal(barrier, inc=1, device_id={"gene": other}, device_id_type=MESH)
    pl.semaphore_wait(barrier, far + 2)

    def request(d):
        return pltpu.make_async_remote_copy(
            src_ref=wanted.at[d - 1], dst_ref=asked_v.at[d - 1],
            send_sem=req_send.at[d - 1], recv_sem=req_recv.at[d - 1],
            device_id={"cell": before(d)}, device_id_type=MESH,
        )

    def blocks(d, side):
        return pltpu.make_async_remote_copy(
            src_ref=out.at[d - 1], dst_ref=inc.at[side, d - 1],
            send_sem=x_send.at[d - 1], recv_sem=x_recv.at[side, d - 1],
            device_id={"cell": after(d)}, device_id_type=MESH,
        )

    def peak(d):
        return pltpu.make_async_remote_copy(
            src_ref=tops, dst_ref=tops_in.at[d - 1],
            send_sem=top_send.at[d - 1], recv_sem=top_recv.at[d - 1],
            device_id={"cell": after(d)}, device_id_type=MESH,
        )

    def slab(c, kind):
        at, size = chunks[c]
        holder = across if kind == 2 else g
        other = across if kind == 0 else sister
        part = a_full.at[holder, pl.ds(at, size)]
        return pltpu.make_async_remote_copy(
            src_ref=part, dst_ref=part,
            send_sem=a_send.at[c, kind], recv_sem=a_recv.at[c, kind],
            device_id={"gene": other}, device_id_type=MESH,
        )

    def each(function):
        def body(d, carry):
            function(d)
            return carry
        lax.fori_loop(1, n, body, 0)

    each(lambda d: request(d).start())

    line = lax.broadcasted_iota(jnp.int32, (rows, BS), 0) + g * rows
    column = lax.broadcasted_iota(jnp.int32, (rows, BS), 1)
    keep = jnp.where(line == column, 0.0, 1.0).astype(jnp.bfloat16)
    for c, (at, size) in enumerate(chunks):
        def place(t, carry, own=at < BLK_DEV):
            tile = aff[meta[t]]
            if own:
                tile = tile * keep
            a_full[g, t] = tile
            return carry
        lax.fori_loop(at, at + size, place, 0)
        slab(c, 0).start()
        slab(c, 1).start()

    each(lambda d: request(d).wait())
    copy = pltpu.make_async_copy(asked_v, asked_s, local_sem)
    copy.start()
    copy.wait()

    def send_blocks(source, side):
        def body(d):
            for r in range(REQ_CAP):
                out[d - 1, r] = source[asked_s[d - 1, 0, r]]
            blocks(d, side).start()
        each(body)

    send_blocks(x_ref, 0)

    def tile_of(t):
        return a_full[:, t].reshape(BS, BS)

    def by_four(function):
        def body(q, carry):
            for j in range(4):
                function(q * 4 + j)
            return carry
        lax.fori_loop(0, BLK_DEV // 4, body, 0)

    def dot(a, b):
        return jnp.dot(a, b, preferred_element_type=jnp.float32)

    def own_part(source):
        def body(i):
            total[i] = dot(tile_of(i), source[i])
        by_four(body)

    def link(k, product):
        chain[k + 1] = product + chain[meta[prev_at + k]]

    chain[0] = jnp.zeros((BS, x_ref.shape[2]), jnp.float32)
    ones = jnp.ones((BS, x_ref.shape[2]), jnp.bfloat16)

    def highest(i, top):
        block = x_ref[i].astype(jnp.float32)
        return jnp.maximum(top, jnp.max(block.reshape(BS // 8, 8, -1), axis=0))

    zero_top = jnp.full((8, x_ref.shape[2]), -jnp.inf, jnp.float32)
    start = lax.fori_loop(0, BLK_DEV, highest, zero_top)
    tops[0:8] = start

    for c in range(len(chunks)):
        slab(c, 0).wait_recv()
        slab(c, 2).start()
    for c in range(len(chunks)):
        slab(c, 1).wait_recv()
        slab(c, 2).wait_recv()

    own_part(x_ref)

    def degree_links(d):
        for r in range(REQ_CAP):
            k = (d - 1) * REQ_CAP + r
            link(k, dot(tile_of(BLK_DEV + k), ones))

    each(degree_links)

    def degree_own(i):
        deg[i] = dot(tile_of(i), ones) + chain[meta[last_at + i]]

    by_four(degree_own)

    for step in range(STEPS):
        side = step % 2
        if step > 0:
            own_part(cur)

        def far_part(d):
            blocks(d, side).wait_recv()
            for r in range(REQ_CAP):
                k = (d - 1) * REQ_CAP + r
                link(k, dot(tile_of(BLK_DEV + k), inc[side, d - 1, r]))

        each(far_part)
        if step < STEPS - 1:
            def settle(i):
                value = (total[i] + chain[meta[last_at + i]]) / deg[i]
                cur[i] = value.astype(jnp.bfloat16)
            by_four(settle)
            each(lambda d: blocks(d, side).wait_send())
            send_blocks(cur, 1 - side)
        else:
            def finish(q, top):
                for j in range(4):
                    i = q * 4 + j
                    value = (total[i] + chain[meta[last_at + i]]) / deg[i]
                    total[i] = value
                    top = jnp.maximum(top, jnp.max(value.reshape(BS // 8, 8, -1), axis=0))
                pltpu.make_async_copy(
                    total.at[pl.ds(q * 4, 4)], last_hbm.at[pl.ds(q * 4, 4)], hbm_sem.at[q]
                ).start()
                return top
            tops[8:16] = lax.fori_loop(0, BLK_DEV // 4, finish, zero_top)

    each(lambda d: peak(d).start())
    each(lambda d: blocks(d, (STEPS - 1) % 2).wait_send())
    for c in range(len(chunks)):
        for kind in range(3):
            slab(c, kind).wait_send()
    each(lambda d: peak(d).wait())

    def join(d, carry):
        return jnp.maximum(carry, tops_in[d - 1])

    best = lax.fori_loop(1, n, join, tops[...])
    top_start = jnp.max(best[0:8], axis=0, keepdims=True)
    top_end = jnp.max(best[8:16], axis=0, keepdims=True)
    ratio[...] = jnp.broadcast_to(top_start / top_end, ratio.shape)

    def drain(q, carry):
        pltpu.make_async_copy(
            total.at[pl.ds(q * 4, 4)], last_hbm.at[pl.ds(q * 4, 4)], hbm_sem.at[q]
        ).wait()
        return carry

    lax.fori_loop(0, BLK_DEV // 4, drain, 0)


def plan(me, n, tile_rows, tile_cols, tile_count):
    links = (n - 1) * REQ_CAP
    count = tile_rows.shape[0]
    order = jnp.arange(count, dtype=jnp.int32)
    valid = order < tile_count[0]
    owner = tile_cols // BLK_DEV
    col_slot = tile_cols - owner * BLK_DEV
    row = tile_rows - me * BLK_DEV
    remote = valid & (owner != me)
    own = valid & (owner == me)
    same = (owner[:, None] == owner[None, :]) & remote[None, :] & (order[None, :] < order[:, None])
    rank = jnp.sum(same.astype(jnp.int32), axis=1)
    k = jnp.where(remote, (jnp.mod(me - owner, n) - 1) * REQ_CAP + rank, -1)
    linked = (row[:, None] == row[None, :]) & remote[None, :] & (k[None, :] < k[:, None])
    prev = jnp.max(jnp.where(linked, k[None, :] + 1, 0), axis=1)
    hit = k[:, None] == jnp.arange(links, dtype=jnp.int32)[None, :]
    mine = row[:, None] == jnp.arange(BLK_DEV, dtype=jnp.int32)[None, :]
    own_tile = jnp.sum(jnp.where(mine & own[:, None], order[:, None], 0), axis=0)
    last = jnp.max(jnp.where(mine & remote[:, None], k[:, None] + 1, 0), axis=0)
    pick = lambda value: jnp.sum(jnp.where(hit, value[:, None], 0), axis=0)
    meta = jnp.concatenate([own_tile, pick(order), pick(prev), last])
    wanted = jnp.pad(pick(col_slot).reshape(n - 1, 1, REQ_CAP), ((0, 0), (0, 7), (0, 128 - REQ_CAP)))
    return meta, wanted


def on_device(n, expression, affinity, tile_rows, tile_cols, tile_count):
    me = lax.axis_index("cell")
    genes = expression.shape[1]
    far = n - 1
    links = far * REQ_CAP
    slots = BLK_DEV + links
    parts = BS // affinity.shape[1]
    meta, wanted = plan(me, n, tile_rows, tile_cols, tile_count)
    n_chunks = len(spans(0, BLK_DEV, 8)) + len(spans(BLK_DEV, slots, max(7, links // 4)))
    bf16, f32, i32 = jnp.bfloat16, jnp.float32, jnp.int32
    dma = pltpu.SemaphoreType.DMA
    vmem = pl.BlockSpec(memory_space=pltpu.VMEM)
    last, ratio = pl.pallas_call(
        functools.partial(kernel, n),
        out_shape=(
            jax.ShapeDtypeStruct((BLK_DEV, BS, genes), f32),
            jax.ShapeDtypeStruct((8, genes), f32),
        ),
        in_specs=[pl.BlockSpec(memory_space=pltpu.SMEM), vmem, vmem, vmem],
        out_specs=(pl.BlockSpec(memory_space=pl.ANY), vmem),
        scratch_shapes=[
            pltpu.VMEM((parts, slots, affinity.shape[1], BS), bf16),
            pltpu.VMEM((BLK_DEV, BS, genes), bf16),
            pltpu.VMEM((BLK_DEV, BS, genes), f32),
            pltpu.VMEM((BLK_DEV, BS, genes), f32),
            pltpu.VMEM((links + 1, BS, genes), f32),
            pltpu.VMEM((2, far, REQ_CAP, BS, genes), bf16),
            pltpu.VMEM((far, REQ_CAP, BS, genes), bf16),
            pltpu.VMEM((far, 8, 128), i32),
            pltpu.SMEM((far, 8, 128), i32),
            pltpu.VMEM((16, genes), f32),
            pltpu.VMEM((far, 16, genes), f32),
            dma((far,)), dma((far,)), dma((far,)), dma((2, far)),
            dma((n_chunks, 3)), dma((n_chunks, 3)), dma((far,)), dma((far,)),
            dma, dma((BLK_DEV // 4,)),
        ],
        compiler_params=pltpu.CompilerParams(
            collective_id=0, has_side_effects=True, vmem_limit_bytes=(62 if n > 8 else 48) * 2**20
        ),
    )(meta, wanted, expression.reshape(BLK_DEV, BS, genes), affinity)
    return last.reshape(BLK_DEV * BS, genes) * ratio[0:1]


def solution(mesh):
    return jax.shard_map(
        functools.partial(on_device, mesh.shape["cell"]),
        mesh=mesh,
        in_specs=(P("cell", "gene"), P("cell", "gene", None), P("cell"), P("cell"), P("cell")),
        out_specs=P("cell", "gene"),
        check_vma=False,
    )
```

```python
import functools
import jax
import jax.numpy as jnp
from jax import lax
from jax.experimental import pallas as pl
from jax.experimental.pallas import tpu as pltpu
from jax.sharding import PartitionSpec as P

BS = 256
BLK_DEV = 32
REQ_CAP = 3
STEPS = 3
MESH = pl.DeviceIdType.MESH


def spans(first, last, size):
    return [(at, min(size, last - at)) for at in range(first, last, size)]


def tile_chunks(links):
    return spans(BLK_DEV, BLK_DEV + links, max(7, links // 4)) + spans(0, BLK_DEV, 4)


def kernel(
    n, meta, wanted, x_hbm, aff_hbm, last_hbm, ratio,
    a_full, aff, cur, total, deg, chain, inc, out, asked_v, asked_s, tops, tops_in,
    req_send, req_recv, x_send, x_recv, a_send, a_recv, top_send, top_recv, local_sem, load_sem, hbm_sem,
):
    far = n - 1
    links = far * REQ_CAP
    slots = BLK_DEV + links
    prev_at = slots
    last_at = slots + links
    chunks = tile_chunks(links)
    me = lax.axis_index("cell")
    g = lax.axis_index("gene")
    across = lax.rem(g + 2, 4)
    sister = g + 1 - 2 * lax.rem(g, 2)
    rows = aff.shape[1]
    genes = cur.shape[2]
    load_aff = pltpu.make_async_copy(aff_hbm, aff, load_sem.at[0])
    load_aff.start()
    load_x = pltpu.make_async_copy(x_hbm, cur, load_sem.at[1])
    load_x.start()

    def after(d):
        return lax.rem(me + d, n)

    def before(d):
        return lax.rem(me + n - d, n)

    barrier = pltpu.get_barrier_semaphore()

    def greet(d, carry):
        pl.semaphore_signal(barrier, inc=1, device_id={"cell": after(d)}, device_id_type=MESH)
        return carry

    lax.fori_loop(1, n, greet, 0)
    for other in (across, sister):
        pl.semaphore_signal(barrier, inc=1, device_id={"gene": other}, device_id_type=MESH)
    pl.semaphore_wait(barrier, far + 2)

    def request(d):
        return pltpu.make_async_remote_copy(
            src_ref=wanted.at[d - 1], dst_ref=asked_v.at[d - 1],
            send_sem=req_send.at[d - 1], recv_sem=req_recv.at[d - 1],
            device_id={"cell": before(d)}, device_id_type=MESH,
        )

    def blocks(d, side):
        return pltpu.make_async_remote_copy(
            src_ref=out.at[d - 1], dst_ref=inc.at[side, d - 1],
            send_sem=x_send.at[d - 1], recv_sem=x_recv.at[side, d - 1],
            device_id={"cell": after(d)}, device_id_type=MESH,
        )

    def peak(d):
        return pltpu.make_async_remote_copy(
            src_ref=tops, dst_ref=tops_in.at[d - 1],
            send_sem=top_send.at[d - 1], recv_sem=top_recv.at[d - 1],
            device_id={"cell": after(d)}, device_id_type=MESH,
        )

    def slab(c, kind):
        at, size = chunks[c]
        holder = across if kind == 2 else g
        other = across if kind == 0 else sister
        part = a_full.at[holder, pl.ds(at, size)]
        return pltpu.make_async_remote_copy(
            src_ref=part, dst_ref=part,
            send_sem=a_send.at[c, kind], recv_sem=a_recv.at[c, kind],
            device_id={"gene": other}, device_id_type=MESH,
        )

    def each(function):
        def body(d, carry):
            function(d)
            return carry
        lax.fori_loop(1, n, body, 0)

    def far_first(function):
        def body(j, carry):
            function(n // 2 + ((j + 1) // 2) * (1 - 2 * lax.rem(j, 2)))
            return carry
        lax.fori_loop(0, far, body, 0)

    def near_first(function):
        def body(q, carry):
            j = far - 1 - q
            function(q, n // 2 + ((j + 1) // 2) * (1 - 2 * lax.rem(j, 2)))
            return carry
        lax.fori_loop(0, far, body, 0)

    each(lambda d: request(d).start())
    load_aff.wait()

    line = lax.broadcasted_iota(jnp.int32, (rows, BS), 0) + g * rows
    column = lax.broadcasted_iota(jnp.int32, (rows, BS), 1)
    keep = jnp.where(line == column, 0.0, 1.0).astype(jnp.bfloat16)
    for c, (at, size) in enumerate(chunks):
        def place(t, carry, own=at < BLK_DEV):
            tile = aff[meta[t]]
            if own:
                tile = tile * keep
            a_full[g, t] = tile
            return carry
        lax.fori_loop(at, at + size, place, 0)
        slab(c, 0).start()
        slab(c, 1).start()

    each(lambda d: request(d).wait())
    copy = pltpu.make_async_copy(asked_v, asked_s, local_sem)
    copy.start()
    copy.wait()
    load_x.wait()

    def send_blocks(source, side):
        def body(d):
            for r in range(REQ_CAP):
                out[d - 1, r] = source[asked_s[d - 1, 0, r]]
            blocks(d, side).start()
        far_first(body)

    send_blocks(cur, 0)

    def tile_of(t):
        return a_full[:, t].reshape(BS, BS)

    def by_four(function):
        def body(q, carry):
            for j in range(4):
                function(q * 4 + j)
            return carry
        lax.fori_loop(0, BLK_DEV // 4, body, 0)

    def dot(a, b):
        return jnp.dot(a, b, preferred_element_type=jnp.float32)

    def own_part():
        def body(i):
            total[i] = dot(tile_of(i), cur[i])
        by_four(body)

    def link(k, product):
        chain[k + 1] = product + chain[meta[prev_at + k]]

    chain[0] = jnp.zeros((BS, genes), jnp.float32)
    ones = jnp.ones((BS, genes), jnp.bfloat16)

    def highest(i, top):
        block = cur[i].astype(jnp.float32)
        return jnp.maximum(top, jnp.max(block.reshape(BS // 8, 8, -1), axis=0))

    zero_top = jnp.full((8, genes), -jnp.inf, jnp.float32)
    start = lax.fori_loop(0, BLK_DEV, highest, zero_top)
    tops[0:8] = start

    def far_degree(k):
        link(k, dot(tile_of(BLK_DEV + k), ones))

    def own_first(i):
        both = dot(tile_of(i), jnp.concatenate([cur[i], ones], axis=1))
        total[i] = both[:, :genes]
        deg[i] = 1.0 / (both[:, genes:] + chain[meta[last_at + i]])

    def use(c):
        at, size = chunks[c]
        slab(c, 1).wait_recv()
        slab(c, 2).wait_recv()
        if at >= BLK_DEV:
            for t in range(at, at + size):
                far_degree(t - BLK_DEV)
        else:
            for t in range(at, at + size):
                own_first(t)

    for c in range(len(chunks)):
        slab(c, 0).wait_recv()
        slab(c, 2).start()
        if c > 0:
            use(c - 1)
    use(len(chunks) - 1)

    for step in range(STEPS):
        side = step % 2
        if step > 0:
            own_part()

        def far_part(q, d):
            blocks(d, side).wait_recv()
            for r in range(REQ_CAP):
                k = q * REQ_CAP + r
                link(k, dot(tile_of(BLK_DEV + k), inc[side, d - 1, r]))

        near_first(far_part)
        if step < STEPS - 1:
            def settle(i):
                value = (total[i] + chain[meta[last_at + i]]) * deg[i]
                cur[i] = value.astype(jnp.bfloat16)
            by_four(settle)
            each(lambda d: blocks(d, side).wait_send())
            send_blocks(cur, 1 - side)
        else:
            def finish(q, top):
                for j in range(4):
                    i = q * 4 + j
                    value = (total[i] + chain[meta[last_at + i]]) * deg[i]
                    total[i] = value
                    top = jnp.maximum(top, jnp.max(value.reshape(BS // 8, 8, -1), axis=0))
                pltpu.make_async_copy(
                    total.at[pl.ds(q * 4, 4)], last_hbm.at[pl.ds(q * 4, 4)], hbm_sem.at[q]
                ).start()
                return top
            tops[8:16] = lax.fori_loop(0, BLK_DEV // 4, finish, zero_top)

    each(lambda d: peak(d).start())
    each(lambda d: blocks(d, (STEPS - 1) % 2).wait_send())
    for c in range(len(chunks)):
        for kind in range(3):
            slab(c, kind).wait_send()
    each(lambda d: peak(d).wait())

    def join(d, carry):
        return jnp.maximum(carry, tops_in[d - 1])

    best = lax.fori_loop(1, n, join, tops[...])
    top_start = jnp.max(best[0:8], axis=0, keepdims=True)
    top_end = jnp.max(best[8:16], axis=0, keepdims=True)
    ratio[...] = jnp.broadcast_to(top_start / top_end, ratio.shape)

    def drain(q, carry):
        pltpu.make_async_copy(
            total.at[pl.ds(q * 4, 4)], last_hbm.at[pl.ds(q * 4, 4)], hbm_sem.at[q]
        ).wait()
        return carry

    lax.fori_loop(0, BLK_DEV // 4, drain, 0)


def plan(me, n, tile_rows, tile_cols, tile_count):
    links = (n - 1) * REQ_CAP
    count = tile_rows.shape[0]
    order = jnp.arange(count, dtype=jnp.int32)
    valid = order < tile_count[0]
    owner = tile_cols // BLK_DEV
    col_slot = tile_cols - owner * BLK_DEV
    row = tile_rows - me * BLK_DEV
    remote = valid & (owner != me)
    own = valid & (owner == me)
    same = (owner[:, None] == owner[None, :]) & remote[None, :] & (order[None, :] < order[:, None])
    rank = jnp.sum(same.astype(jnp.int32), axis=1)
    d = jnp.mod(me - owner, n)
    turn = (n - 2) - jnp.where(d > n // 2, 2 * (d - n // 2), jnp.maximum(n - 2 * d - 1, 0))
    k = jnp.where(remote, turn * REQ_CAP + rank, -1)
    asked = jnp.where(remote, (d - 1) * REQ_CAP + rank, -1)
    linked = (row[:, None] == row[None, :]) & remote[None, :] & (k[None, :] < k[:, None])
    prev = jnp.max(jnp.where(linked, k[None, :] + 1, 0), axis=1)
    every = jnp.arange(links, dtype=jnp.int32)[None, :]
    mine = row[:, None] == jnp.arange(BLK_DEV, dtype=jnp.int32)[None, :]
    own_tile = jnp.sum(jnp.where(mine & own[:, None], order[:, None], 0), axis=0)
    last = jnp.max(jnp.where(mine & remote[:, None], k[:, None] + 1, 0), axis=0)
    pick = lambda at, value: jnp.sum(jnp.where(at[:, None] == every, value[:, None], 0), axis=0)
    meta = jnp.concatenate([own_tile, pick(k, order), pick(k, prev), last])
    wanted = jnp.pad(pick(asked, col_slot).reshape(n - 1, 1, REQ_CAP), ((0, 0), (0, 7), (0, 128 - REQ_CAP)))
    return meta, wanted


def on_device(n, expression, affinity, tile_rows, tile_cols, tile_count):
    me = lax.axis_index("cell")
    genes = expression.shape[1]
    far = n - 1
    links = far * REQ_CAP
    slots = BLK_DEV + links
    parts = BS // affinity.shape[1]
    meta, wanted = plan(me, n, tile_rows, tile_cols, tile_count)
    n_chunks = len(tile_chunks(links))
    bf16, f32, i32 = jnp.bfloat16, jnp.float32, jnp.int32
    dma = pltpu.SemaphoreType.DMA
    anywhere = pl.BlockSpec(memory_space=pl.ANY)
    vmem = pl.BlockSpec(memory_space=pltpu.VMEM)
    last, ratio = pl.pallas_call(
        functools.partial(kernel, n),
        out_shape=(
            jax.ShapeDtypeStruct((BLK_DEV, BS, genes), f32),
            jax.ShapeDtypeStruct((8, genes), f32),
        ),
        in_specs=[pl.BlockSpec(memory_space=pltpu.SMEM), vmem, anywhere, anywhere],
        out_specs=(anywhere, vmem),
        scratch_shapes=[
            pltpu.VMEM((parts, slots, affinity.shape[1], BS), bf16),
            pltpu.VMEM(affinity.shape, bf16),
            pltpu.VMEM((BLK_DEV, BS, genes), bf16),
            pltpu.VMEM((BLK_DEV, BS, genes), f32),
            pltpu.VMEM((BLK_DEV, BS, genes), f32),
            pltpu.VMEM((links + 1, BS, genes), f32),
            pltpu.VMEM((2, far, REQ_CAP, BS, genes), bf16),
            pltpu.VMEM((far, REQ_CAP, BS, genes), bf16),
            pltpu.VMEM((far, 8, 128), i32),
            pltpu.SMEM((far, 8, 128), i32),
            pltpu.VMEM((16, genes), f32),
            pltpu.VMEM((far, 16, genes), f32),
            dma((far,)), dma((far,)), dma((far,)), dma((2, far)),
            dma((n_chunks, 3)), dma((n_chunks, 3)), dma((far,)), dma((far,)),
            dma, dma((2,)), dma((BLK_DEV // 4,)),
        ],
        compiler_params=pltpu.CompilerParams(
            collective_id=0, has_side_effects=True, vmem_limit_bytes=(62 if n > 8 else 48) * 2**20
        ),
    )(meta, wanted, expression.reshape(BLK_DEV, BS, genes), affinity)
    return last.reshape(BLK_DEV * BS, genes) * ratio[0:1]


def solution(mesh):
    return jax.shard_map(
        functools.partial(on_device, mesh.shape["cell"]),
        mesh=mesh,
        in_specs=(P("cell", "gene"), P("cell", "gene", None), P("cell"), P("cell"), P("cell")),
        out_specs=P("cell", "gene"),
        check_vma=False,
    )
```

```python
import functools
import jax
import jax.numpy as jnp
from jax import lax
from jax.experimental import pallas as pl
from jax.experimental.pallas import tpu as pltpu
from jax.sharding import PartitionSpec as P

BS = 256
BLK_DEV = 32
REQ_CAP = 3
STEPS = 3
MESH = pl.DeviceIdType.MESH


def spans(first, last, size):
    return [(at, min(size, last - at)) for at in range(first, last, size)]


def tile_chunks(links):
    return spans(BLK_DEV, BLK_DEV + links, max(7, links // 4)) + spans(0, BLK_DEV, 4)


def kernel(
    n, meta, wanted, x_hbm, aff_hbm, last_hbm, ratio,
    a_full, aff, cur, total, deg, chain, inc, out, asked_v, asked_s, tops, tops_in,
    req_send, req_recv, x_send, x_recv, a_send, a_recv, top_send, top_recv, local_sem, load_sem, hbm_sem,
):
    far = n - 1
    links = far * REQ_CAP
    slots = BLK_DEV + links
    prev_at = slots
    last_at = slots + links
    chunks = tile_chunks(links)
    me = lax.axis_index("cell")
    g = lax.axis_index("gene")
    across = lax.rem(g + 2, 4)
    sister = g + 1 - 2 * lax.rem(g, 2)
    rows = aff.shape[1]
    genes = cur.shape[2]
    load_aff = pltpu.make_async_copy(aff_hbm, aff, load_sem.at[0])
    load_aff.start()
    load_x = pltpu.make_async_copy(x_hbm, cur, load_sem.at[1])
    load_x.start()

    def after(d):
        return lax.rem(me + d, n)

    def before(d):
        return lax.rem(me + n - d, n)

    barrier = pltpu.get_barrier_semaphore()

    def greet(d, carry):
        pl.semaphore_signal(barrier, inc=1, device_id={"cell": after(d)}, device_id_type=MESH)
        return carry

    lax.fori_loop(1, n, greet, 0)
    for other in (across, sister):
        pl.semaphore_signal(barrier, inc=1, device_id={"gene": other}, device_id_type=MESH)
    pl.semaphore_wait(barrier, far + 2)

    def request(d):
        return pltpu.make_async_remote_copy(
            src_ref=wanted.at[d - 1], dst_ref=asked_v.at[d - 1],
            send_sem=req_send.at[d - 1], recv_sem=req_recv.at[d - 1],
            device_id={"cell": before(d)}, device_id_type=MESH,
        )

    def blocks(d, side):
        return pltpu.make_async_remote_copy(
            src_ref=out.at[d - 1], dst_ref=inc.at[side, d - 1],
            send_sem=x_send.at[d - 1], recv_sem=x_recv.at[side, d - 1],
            device_id={"cell": after(d)}, device_id_type=MESH,
        )

    def peak(d):
        return pltpu.make_async_remote_copy(
            src_ref=tops, dst_ref=tops_in.at[d - 1],
            send_sem=top_send.at[d - 1], recv_sem=top_recv.at[d - 1],
            device_id={"cell": after(d)}, device_id_type=MESH,
        )

    def slab(c, kind):
        at, size = chunks[c]
        holder = across if kind == 2 else g
        other = across if kind == 0 else sister
        part = a_full.at[holder, pl.ds(at, size)]
        return pltpu.make_async_remote_copy(
            src_ref=part, dst_ref=part,
            send_sem=a_send.at[c, kind], recv_sem=a_recv.at[c, kind],
            device_id={"gene": other}, device_id_type=MESH,
        )

    def each(function):
        def body(d, carry):
            function(d)
            return carry
        lax.fori_loop(1, n, body, 0)

    def far_first(function):
        def body(j, carry):
            function(n // 2 + ((j + 1) // 2) * (1 - 2 * lax.rem(j, 2)))
            return carry
        lax.fori_loop(0, far, body, 0)

    def near_first(function):
        def body(q, carry):
            j = far - 1 - q
            function(q, n // 2 + ((j + 1) // 2) * (1 - 2 * lax.rem(j, 2)))
            return carry
        lax.fori_loop(0, far, body, 0)

    each(lambda d: request(d).start())
    load_aff.wait()

    line = lax.broadcasted_iota(jnp.int32, (rows, BS), 0) + g * rows
    column = lax.broadcasted_iota(jnp.int32, (rows, BS), 1)
    keep = jnp.where(line == column, 0.0, 1.0).astype(jnp.bfloat16)
    for c, (at, size) in enumerate(chunks):
        def place(t, carry, own=at < BLK_DEV):
            tile = aff[meta[t]]
            if own:
                tile = tile * keep
            a_full[g, t] = tile
            return carry
        lax.fori_loop(at, at + size, place, 0)
        slab(c, 0).start()
        slab(c, 1).start()

    each(lambda d: request(d).wait())
    copy = pltpu.make_async_copy(asked_v, asked_s, local_sem)
    copy.start()
    copy.wait()
    load_x.wait()

    def send_blocks(source, side):
        def body(d):
            for r in range(REQ_CAP):
                out[d - 1, r] = source[asked_s[d - 1, 0, r]]
            blocks(d, side).start()
        far_first(body)

    send_blocks(cur, 0)

    def tile_of(t):
        return a_full[:, t].reshape(BS, BS)

    def by_four(function):
        def body(q, carry):
            for j in range(4):
                function(q * 4 + j)
            return carry
        lax.fori_loop(0, BLK_DEV // 4, body, 0)

    def dot(a, b):
        return jnp.dot(a, b, preferred_element_type=jnp.float32)

    def own_part():
        def body(i):
            total[i] = dot(tile_of(i), cur[i])
        by_four(body)

    def link(k, product):
        chain[k + 1] = product + chain[meta[prev_at + k]]

    chain[0] = jnp.zeros((BS, genes), jnp.float32)
    ones = jnp.ones((BS, genes), jnp.bfloat16)

    def highest(i, top):
        block = cur[i].astype(jnp.float32)
        return jnp.maximum(top, jnp.max(block.reshape(BS // 8, 8, -1), axis=0))

    zero_top = jnp.full((8, genes), -jnp.inf, jnp.float32)
    start = lax.fori_loop(0, BLK_DEV, highest, zero_top)
    tops[0:8] = start

    def far_degree(k):
        link(k, dot(tile_of(BLK_DEV + k), ones))

    def own_first(i):
        both = dot(tile_of(i), jnp.concatenate([cur[i], ones], axis=1))
        total[i] = both[:, :genes]
        deg[i] = 1.0 / (both[:, genes:] + chain[meta[last_at + i]])

    def use(c):
        at, size = chunks[c]
        slab(c, 1).wait_recv()
        slab(c, 2).wait_recv()
        if at >= BLK_DEV:
            for t in range(at, at + size):
                far_degree(t - BLK_DEV)
        else:
            for t in range(at, at + size):
                own_first(t)

    for c in range(len(chunks)):
        slab(c, 0).wait_recv()
        slab(c, 2).start()
        if c > 0:
            use(c - 1)
    use(len(chunks) - 1)

    for step in range(STEPS):
        side = step % 2
        if step > 0:
            own_part()

        def far_part(q, d):
            blocks(d, side).wait_recv()
            for r in range(REQ_CAP):
                k = q * REQ_CAP + r
                link(k, dot(tile_of(BLK_DEV + k), inc[side, d - 1, r]))

        near_first(far_part)
        if step < STEPS - 1:
            def settle(i):
                value = (total[i] + chain[meta[last_at + i]]) * deg[i]
                cur[i] = value.astype(jnp.bfloat16)
            by_four(settle)
            each(lambda d: blocks(d, side).wait_send())
            send_blocks(cur, 1 - side)
        else:
            def finish(q, top):
                for j in range(4):
                    i = q * 4 + j
                    value = (total[i] + chain[meta[last_at + i]]) * deg[i]
                    total[i] = value
                    top = jnp.maximum(top, jnp.max(value.reshape(BS // 8, 8, -1), axis=0))
                pltpu.make_async_copy(
                    total.at[pl.ds(q * 4, 4)], last_hbm.at[pl.ds(q * 4, 4)], hbm_sem.at[q]
                ).start()
                return top
            tops[8:16] = lax.fori_loop(0, BLK_DEV // 4, finish, zero_top)

    each(lambda d: peak(d).start())
    each(lambda d: blocks(d, (STEPS - 1) % 2).wait_send())
    for c in range(len(chunks)):
        for kind in range(3):
            slab(c, kind).wait_send()
    each(lambda d: peak(d).wait())

    def join(d, carry):
        return jnp.maximum(carry, tops_in[d - 1])

    best = lax.fori_loop(1, n, join, tops[...])
    top_start = jnp.max(best[0:8], axis=0, keepdims=True)
    top_end = jnp.max(best[8:16], axis=0, keepdims=True)
    ratio[...] = jnp.broadcast_to(top_start / top_end, ratio.shape)

    def drain(q, carry):
        pltpu.make_async_copy(
            total.at[pl.ds(q * 4, 4)], last_hbm.at[pl.ds(q * 4, 4)], hbm_sem.at[q]
        ).wait()
        return carry

    lax.fori_loop(0, BLK_DEV // 4, drain, 0)


def rescale(ratio, last, scaled):
    scaled[...] = last[...] * ratio[0:1]


def plan(me, n, tile_rows, tile_cols, tile_count):
    links = (n - 1) * REQ_CAP
    count = tile_rows.shape[0]
    order = jnp.arange(count, dtype=jnp.int32)
    valid = order < tile_count[0]
    owner = tile_cols // BLK_DEV
    col_slot = tile_cols - owner * BLK_DEV
    row = tile_rows - me * BLK_DEV
    remote = valid & (owner != me)
    own = valid & (owner == me)
    same = (owner[:, None] == owner[None, :]) & remote[None, :] & (order[None, :] < order[:, None])
    rank = jnp.sum(same.astype(jnp.int32), axis=1)
    d = jnp.mod(me - owner, n)
    turn = (n - 2) - jnp.where(d > n // 2, 2 * (d - n // 2), jnp.maximum(n - 2 * d - 1, 0))
    k = jnp.where(remote, turn * REQ_CAP + rank, -1)
    asked = jnp.where(remote, (d - 1) * REQ_CAP + rank, -1)
    linked = (row[:, None] == row[None, :]) & remote[None, :] & (k[None, :] < k[:, None])
    prev = jnp.max(jnp.where(linked, k[None, :] + 1, 0), axis=1)
    every = jnp.arange(links, dtype=jnp.int32)[None, :]
    mine = row[:, None] == jnp.arange(BLK_DEV, dtype=jnp.int32)[None, :]
    own_tile = jnp.sum(jnp.where(mine & own[:, None], order[:, None], 0), axis=0)
    last = jnp.max(jnp.where(mine & remote[:, None], k[:, None] + 1, 0), axis=0)
    pick = lambda at, value: jnp.sum(jnp.where(at[:, None] == every, value[:, None], 0), axis=0)
    meta = jnp.concatenate([own_tile, pick(k, order), pick(k, prev), last])
    wanted = jnp.pad(pick(asked, col_slot).reshape(n - 1, 1, REQ_CAP), ((0, 0), (0, 7), (0, 128 - REQ_CAP)))
    return meta, wanted


def on_device(n, expression, affinity, tile_rows, tile_cols, tile_count):
    me = lax.axis_index("cell")
    genes = expression.shape[1]
    far = n - 1
    links = far * REQ_CAP
    slots = BLK_DEV + links
    parts = BS // affinity.shape[1]
    meta, wanted = plan(me, n, tile_rows, tile_cols, tile_count)
    n_chunks = len(tile_chunks(links))
    bf16, f32, i32 = jnp.bfloat16, jnp.float32, jnp.int32
    dma = pltpu.SemaphoreType.DMA
    anywhere = pl.BlockSpec(memory_space=pl.ANY)
    vmem = pl.BlockSpec(memory_space=pltpu.VMEM)
    last, ratio = pl.pallas_call(
        functools.partial(kernel, n),
        out_shape=(
            jax.ShapeDtypeStruct((BLK_DEV, BS, genes), f32),
            jax.ShapeDtypeStruct((8, genes), f32),
        ),
        in_specs=[pl.BlockSpec(memory_space=pltpu.SMEM), vmem, anywhere, anywhere],
        out_specs=(anywhere, vmem),
        scratch_shapes=[
            pltpu.VMEM((parts, slots, affinity.shape[1], BS), bf16),
            pltpu.VMEM(affinity.shape, bf16),
            pltpu.VMEM((BLK_DEV, BS, genes), bf16),
            pltpu.VMEM((BLK_DEV, BS, genes), f32),
            pltpu.VMEM((BLK_DEV, BS, genes), f32),
            pltpu.VMEM((links + 1, BS, genes), f32),
            pltpu.VMEM((2, far, REQ_CAP, BS, genes), bf16),
            pltpu.VMEM((far, REQ_CAP, BS, genes), bf16),
            pltpu.VMEM((far, 8, 128), i32),
            pltpu.SMEM((far, 8, 128), i32),
            pltpu.VMEM((16, genes), f32),
            pltpu.VMEM((far, 16, genes), f32),
            dma((far,)), dma((far,)), dma((far,)), dma((2, far)),
            dma((n_chunks, 3)), dma((n_chunks, 3)), dma((far,)), dma((far,)),
            dma, dma((2,)), dma((BLK_DEV // 4,)),
        ],
        compiler_params=pltpu.CompilerParams(
            collective_id=0, has_side_effects=True, vmem_limit_bytes=62 * 2**20
        ),
    )(meta, wanted, expression.reshape(BLK_DEV, BS, genes), affinity)
    scaled = pl.pallas_call(
        rescale,
        grid=(8,),
        out_shape=jax.ShapeDtypeStruct((BLK_DEV * BS, genes), f32),
        in_specs=[
            pl.BlockSpec((8, genes), lambda q: (0, 0)),
            pl.BlockSpec((BLK_DEV * BS // 8, genes), lambda q: (q, 0)),
        ],
        out_specs=pl.BlockSpec((BLK_DEV * BS // 8, genes), lambda q: (q, 0)),
        compiler_params=pltpu.CompilerParams(vmem_limit_bytes=32 * 2**20),
    )(ratio, last.reshape(BLK_DEV * BS, genes))
    return scaled


def solution(mesh):
    return jax.shard_map(
        functools.partial(on_device, mesh.shape["cell"]),
        mesh=mesh,
        in_specs=(P("cell", "gene"), P("cell", "gene", None), P("cell"), P("cell"), P("cell")),
        out_specs=P("cell", "gene"),
        check_vma=False,
    )
```

```python
import functools
import jax
import jax.numpy as jnp
from jax import lax
from jax.experimental import pallas as pl
from jax.experimental.pallas import tpu as pltpu
from jax.sharding import PartitionSpec as P

BS = 256
BLK_DEV = 32
REQ_CAP = 3
STEPS = 3
MESH = pl.DeviceIdType.MESH


def spans(first, last, size):
    return [(at, min(size, last - at)) for at in range(first, last, size)]


def tile_chunks(links):
    return spans(BLK_DEV, BLK_DEV + links, max(7, links // 4)) + spans(0, BLK_DEV, 4)


def kernel(
    n, meta, wanted, x_hbm, aff_hbm, last_hbm, ratio,
    a_full, aff, cur, total, deg, chain, inc, out, asked_v, asked_s, tops, tops_in,
    req_send, req_recv, x_send, x_recv, a_send, a_recv, top_send, top_recv, local_sem, load_sem, hbm_sem,
):
    far = n - 1
    links = far * REQ_CAP
    slots = BLK_DEV + links
    prev_at = slots
    last_at = slots + links
    chunks = tile_chunks(links)
    me = lax.axis_index("cell")
    g = lax.axis_index("gene")
    across = lax.rem(g + 2, 4)
    sister = g + 1 - 2 * lax.rem(g, 2)
    rows = aff.shape[1]
    genes = cur.shape[2]
    load_aff = pltpu.make_async_copy(aff_hbm, aff, load_sem.at[0])
    load_aff.start()
    load_x = pltpu.make_async_copy(x_hbm, cur, load_sem.at[1])
    load_x.start()

    def after(d):
        return lax.rem(me + d, n)

    def before(d):
        return lax.rem(me + n - d, n)

    barrier = pltpu.get_barrier_semaphore()

    def greet(d, carry):
        pl.semaphore_signal(barrier, inc=1, device_id={"cell": after(d)}, device_id_type=MESH)
        return carry

    lax.fori_loop(1, n, greet, 0)
    for other in (across, sister):
        pl.semaphore_signal(barrier, inc=1, device_id={"gene": other}, device_id_type=MESH)
    pl.semaphore_wait(barrier, far + 2)

    def request(d):
        return pltpu.make_async_remote_copy(
            src_ref=wanted.at[d - 1], dst_ref=asked_v.at[d - 1],
            send_sem=req_send.at[d - 1], recv_sem=req_recv.at[d - 1],
            device_id={"cell": before(d)}, device_id_type=MESH,
        )

    def blocks(d, side):
        return pltpu.make_async_remote_copy(
            src_ref=out.at[d - 1], dst_ref=inc.at[side, d - 1],
            send_sem=x_send.at[d - 1], recv_sem=x_recv.at[side, d - 1],
            device_id={"cell": after(d)}, device_id_type=MESH,
        )

    def peak(d):
        return pltpu.make_async_remote_copy(
            src_ref=tops, dst_ref=tops_in.at[d - 1],
            send_sem=top_send.at[d - 1], recv_sem=top_recv.at[d - 1],
            device_id={"cell": after(d)}, device_id_type=MESH,
        )

    def slab(c, kind):
        at, size = chunks[c]
        holder = across if kind == 2 else g
        other = across if kind == 0 else sister
        part = a_full.at[holder, pl.ds(at, size)]
        return pltpu.make_async_remote_copy(
            src_ref=part, dst_ref=part,
            send_sem=a_send.at[c, kind], recv_sem=a_recv.at[c, kind],
            device_id={"gene": other}, device_id_type=MESH,
        )

    def each(function):
        def body(d, carry):
            function(d)
            return carry
        lax.fori_loop(1, n, body, 0)

    def far_first(function):
        def body(j, carry):
            function(n // 2 + ((j + 1) // 2) * (1 - 2 * lax.rem(j, 2)))
            return carry
        lax.fori_loop(0, far, body, 0)

    def near_first(function):
        def body(q, carry):
            j = far - 1 - q
            function(q, n // 2 + ((j + 1) // 2) * (1 - 2 * lax.rem(j, 2)))
            return carry
        lax.fori_loop(0, far, body, 0)

    each(lambda d: request(d).start())
    load_aff.wait()

    line = lax.broadcasted_iota(jnp.int32, (rows, BS), 0) + g * rows
    column = lax.broadcasted_iota(jnp.int32, (rows, BS), 1)
    keep = jnp.where(line == column, 0.0, 1.0).astype(jnp.bfloat16)
    for c, (at, size) in enumerate(chunks):
        def place(t, carry, own=at < BLK_DEV):
            tile = aff[meta[t]]
            if own:
                tile = tile * keep
            a_full[g, t] = tile
            return carry
        lax.fori_loop(at, at + size, place, 0)
        slab(c, 0).start()
        slab(c, 1).start()

    each(lambda d: request(d).wait())
    copy = pltpu.make_async_copy(asked_v, asked_s, local_sem)
    copy.start()
    copy.wait()
    load_x.wait()

    def send_blocks(source, side):
        def body(d):
            for r in range(REQ_CAP):
                out[d - 1, r] = source[asked_s[d - 1, 0, r]]
            blocks(d, side).start()
        far_first(body)

    send_blocks(cur, 0)

    def tile_of(t):
        return a_full[:, t].reshape(BS, BS)

    def by_four(function):
        def body(q, carry):
            for j in range(4):
                function(q * 4 + j)
            return carry
        lax.fori_loop(0, BLK_DEV // 4, body, 0)

    def dot(a, b):
        return jnp.dot(a, b, preferred_element_type=jnp.float32)

    def own_part():
        def body(i):
            total[i] = dot(tile_of(i), cur[i])
        by_four(body)

    def link(k, product):
        chain[k + 1] = product + chain[meta[prev_at + k]]

    chain[0] = jnp.zeros((BS, genes), jnp.float32)
    ones = jnp.ones((BS, genes), jnp.bfloat16)

    def highest(i, top):
        block = cur[i].astype(jnp.float32)
        return jnp.maximum(top, jnp.max(block.reshape(BS // 8, 8, -1), axis=0))

    zero_top = jnp.full((8, genes), -jnp.inf, jnp.float32)
    start = lax.fori_loop(0, BLK_DEV, highest, zero_top)
    tops[0:8] = start

    def far_degree(k):
        link(k, dot(tile_of(BLK_DEV + k), ones))

    def own_first(i):
        both = dot(tile_of(i), jnp.concatenate([cur[i], ones], axis=1))
        total[i] = both[:, :genes]
        deg[i] = 1.0 / (both[:, genes:] + chain[meta[last_at + i]])

    def use(c):
        at, size = chunks[c]
        slab(c, 1).wait_recv()
        slab(c, 2).wait_recv()
        if at >= BLK_DEV:
            for t in range(at, at + size):
                far_degree(t - BLK_DEV)
        else:
            for t in range(at, at + size):
                own_first(t)

    for c in range(len(chunks)):
        slab(c, 0).wait_recv()
        slab(c, 2).start()
        if c > 0:
            use(c - 1)
    use(len(chunks) - 1)

    for step in range(STEPS):
        side = step % 2
        if step > 0:
            own_part()

        def far_part(q, d):
            blocks(d, side).wait_recv()
            for r in range(REQ_CAP):
                k = q * REQ_CAP + r
                link(k, dot(tile_of(BLK_DEV + k), inc[side, d - 1, r]))

        near_first(far_part)
        if step < STEPS - 1:
            def settle(i):
                value = (total[i] + chain[meta[last_at + i]]) * deg[i]
                cur[i] = value.astype(jnp.bfloat16)
            by_four(settle)
            each(lambda d: blocks(d, side).wait_send())
            send_blocks(cur, 1 - side)
        else:
            def finish(q, top):
                for j in range(4):
                    i = q * 4 + j
                    value = (total[i] + chain[meta[last_at + i]]) * deg[i]
                    total[i] = value
                    top = jnp.maximum(top, jnp.max(value.reshape(BS // 8, 8, -1), axis=0))
                pltpu.make_async_copy(
                    total.at[pl.ds(q * 4, 4)], last_hbm.at[pl.ds(q * 4, 4)], hbm_sem.at[q]
                ).start()
                return top
            tops[8:16] = lax.fori_loop(0, BLK_DEV // 4, finish, zero_top)

    each(lambda d: peak(d).start())
    each(lambda d: blocks(d, (STEPS - 1) % 2).wait_send())
    for c in range(len(chunks)):
        for kind in range(3):
            slab(c, kind).wait_send()
    each(lambda d: peak(d).wait())

    def join(d, carry):
        return jnp.maximum(carry, tops_in[d - 1])

    best = lax.fori_loop(1, n, join, tops[...])
    top_start = jnp.max(best[0:8], axis=0, keepdims=True)
    top_end = jnp.max(best[8:16], axis=0, keepdims=True)
    ratio[...] = jnp.broadcast_to(top_start / top_end, ratio.shape)

    def drain(q, carry):
        pltpu.make_async_copy(
            total.at[pl.ds(q * 4, 4)], last_hbm.at[pl.ds(q * 4, 4)], hbm_sem.at[q]
        ).wait()
        return carry

    lax.fori_loop(0, BLK_DEV // 4, drain, 0)


def rescale(ratio, last, scaled):
    scaled[...] = last[...] * ratio[0:1]


def plan(me, n, tile_rows, tile_cols, tile_count):
    links = (n - 1) * REQ_CAP
    count = tile_rows.shape[0]
    order = jnp.arange(count, dtype=jnp.int32)
    valid = order < tile_count[0]
    owner = tile_cols // BLK_DEV
    col_slot = tile_cols - owner * BLK_DEV
    row = tile_rows - me * BLK_DEV
    remote = valid & (owner != me)
    own = valid & (owner == me)
    same = (owner[:, None] == owner[None, :]) & remote[None, :] & (order[None, :] < order[:, None])
    rank = jnp.sum(same.astype(jnp.int32), axis=1)
    d = jnp.mod(me - owner, n)
    turn = (n - 2) - jnp.where(d > n // 2, 2 * (d - n // 2), jnp.maximum(n - 2 * d - 1, 0))
    k = jnp.where(remote, turn * REQ_CAP + rank, -1)
    asked = jnp.where(remote, (d - 1) * REQ_CAP + rank, -1)
    linked = (row[:, None] == row[None, :]) & remote[None, :] & (k[None, :] < k[:, None])
    prev = jnp.max(jnp.where(linked, k[None, :] + 1, 0), axis=1)
    every = jnp.arange(links, dtype=jnp.int32)[None, :]
    mine = row[:, None] == jnp.arange(BLK_DEV, dtype=jnp.int32)[None, :]
    own_tile = jnp.sum(jnp.where(mine & own[:, None], order[:, None], 0), axis=0)
    last = jnp.max(jnp.where(mine & remote[:, None], k[:, None] + 1, 0), axis=0)
    pick = lambda at, value: jnp.sum(jnp.where(at[:, None] == every, value[:, None], 0), axis=0)
    meta = jnp.concatenate([own_tile, pick(k, order), pick(k, prev), last])
    wanted = jnp.pad(pick(asked, col_slot).reshape(n - 1, 1, REQ_CAP), ((0, 0), (0, 7), (0, 128 - REQ_CAP)))
    return meta, wanted


def on_device(n, expression, affinity, tile_rows, tile_cols, tile_count):
    me = lax.axis_index("cell")
    genes = expression.shape[1]
    far = n - 1
    links = far * REQ_CAP
    slots = BLK_DEV + links
    parts = BS // affinity.shape[1]
    meta, wanted = plan(me, n, tile_rows, tile_cols, tile_count)
    n_chunks = len(tile_chunks(links))
    bf16, f32, i32 = jnp.bfloat16, jnp.float32, jnp.int32
    dma = pltpu.SemaphoreType.DMA
    anywhere = pl.BlockSpec(memory_space=pl.ANY)
    vmem = pl.BlockSpec(memory_space=pltpu.VMEM)
    last, ratio = pl.pallas_call(
        functools.partial(kernel, n),
        out_shape=(
            jax.ShapeDtypeStruct((BLK_DEV, BS, genes), f32),
            jax.ShapeDtypeStruct((8, genes), f32),
        ),
        in_specs=[pl.BlockSpec(memory_space=pltpu.SMEM), vmem, anywhere, anywhere],
        out_specs=(anywhere, vmem),
        scratch_shapes=[
            pltpu.VMEM((parts, slots, affinity.shape[1], BS), bf16),
            pltpu.VMEM(affinity.shape, bf16),
            pltpu.VMEM((BLK_DEV, BS, genes), bf16),
            pltpu.VMEM((BLK_DEV, BS, genes), f32),
            pltpu.VMEM((BLK_DEV, BS, genes), f32),
            pltpu.VMEM((links + 1, BS, genes), f32),
            pltpu.VMEM((2, far, REQ_CAP, BS, genes), bf16),
            pltpu.VMEM((far, REQ_CAP, BS, genes), bf16),
            pltpu.VMEM((far, 8, 128), i32),
            pltpu.SMEM((far, 8, 128), i32),
            pltpu.VMEM((16, genes), f32),
            pltpu.VMEM((far, 16, genes), f32),
            dma((far,)), dma((far,)), dma((far,)), dma((2, far)),
            dma((n_chunks, 3)), dma((n_chunks, 3)), dma((far,)), dma((far,)),
            dma, dma((2,)), dma((BLK_DEV // 4,)),
        ],
        compiler_params=pltpu.CompilerParams(
            collective_id=0, has_side_effects=True, vmem_limit_bytes=62 * 2**20
        ),
    )(meta, wanted, expression.reshape(BLK_DEV, BS, genes), affinity)
    scaled = pl.pallas_call(
        rescale,
        grid=(8,),
        out_shape=jax.ShapeDtypeStruct((BLK_DEV * BS, genes), f32),
        in_specs=[
            pl.BlockSpec((8, genes), lambda q: (0, 0)),
            pl.BlockSpec((BLK_DEV * BS // 8, genes), lambda q: (q, 0)),
        ],
        out_specs=pl.BlockSpec((BLK_DEV * BS // 8, genes), lambda q: (q, 0)),
        compiler_params=pltpu.CompilerParams(vmem_limit_bytes=62 * 2**20),
    )(ratio, last.reshape(BLK_DEV * BS, genes))
    return scaled


def solution(mesh):
    return jax.shard_map(
        functools.partial(on_device, mesh.shape["cell"]),
        mesh=mesh,
        in_specs=(P("cell", "gene"), P("cell", "gene", None), P("cell"), P("cell"), P("cell")),
        out_specs=P("cell", "gene"),
        check_vma=False,
    )
```
